32 devices in a mesh: space: 8 (over z, y), dp: 4 (over x, core).
Axes of the slice: x: 2, y: 2, z: 4, core: 2. Of those that a mesh axis runs over, the one named last changes fastest.
Arguments:
- input_states: bfloat16 [4, 8, 200, 1024], P('dp', 'space'), may hold values from -6 to 6
- loss_sensitivity: bfloat16 [4, 8, 200, 1024], P('dp', 'space'), may hold values from -6 to 6
- ocean: int32 [8, 1024], P('space'), may hold values 0 or 1
- neighbours: int32 [8, 8], P('space'), may hold values from -1 to 7, as said below
- fold_flag: int32 [8], P('space'), may hold values from 0 to 1, as said below
- w_first: bfloat16 [9, 200, 200], replicated, may hold values from -0.125 to 0.125
- w_second: bfloat16 [9, 200, 200], replicated, may hold values from -0.125 to 0.125
Outputs:
- prediction: bfloat16 [4, 8, 200, 1024], P('dp', 'space')
- earlier_kernel_slope: float32 [9, 200, 200], replicated
- latter_kernel_slope: float32 [9, 200, 200], replicated
The draws below stay inside these ranges and needn't reach their ends.
Inputs may be any that keep to these rules, and one draw needn't show every extreme that they name: Tiles sit on a grid of 2 x 16 tile positions, some of them land; the ocean tiles carry numbers 0 to 7 in no particular order of positions; longitude wraps; the top row's northern neighbour is the mirrored tile of the same row (fold_flag 1) and its diagonal northern neighbours are -1. The relation is symmetric: if u is t's neighbour in one direction, t is u's in the opposite one (north for north across the fold). `fold_flag`: 1 exactly for tiles of the top tile row.
All inputs are finite; a program needn't handle non-finite values. No bound on the sum of `ocean` on one device may be relied on, other than what follows from the above.
Results may differ from the reference program's by a relative error of at most 0.005.
Values may be sent and summed in bfloat16 or wider, within the bound.
A program may use at most 64 MiB of HBM per device.

```python
import jax
import jax.numpy as jnp
from jax import lax

CH = 200
SIDE = 32
GRID_COLS = 16
TILES = 8
GRID_ROWS = 2
N_DP = 4


def tile_layout(key):
    rows = GRID_ROWS
    cols = GRID_COLS
    total = rows * cols
    order = jax.random.permutation(jax.random.fold_in(key, 11), total)
    ranking = jnp.zeros((total,), jnp.int32).at[order].set(jnp.arange(total, dtype=jnp.int32))
    ocean_pos = (ranking < TILES).astype(jnp.int32)
    tile_of_pos = jnp.where(ocean_pos == 1, jnp.cumsum(ocean_pos) - 1, -1).astype(jnp.int32)
    position = jnp.argsort(1 - ocean_pos, stable=True)[:TILES].astype(jnp.int32)
    row = position // cols
    col = position % cols
    top = row == rows - 1

    def lookup(r, c, allowed):
        spot = jnp.clip(r * cols + c % cols, 0, total - 1)
        return jnp.where(allowed, tile_of_pos[spot], -1)
    everywhere = jnp.ones_like(top)
    north = jnp.where(top, lookup(row, cols - 1 - col, everywhere), lookup(row + 1, col, everywhere))
    south = lookup(row - 1, col, row >= 1)
    east = lookup(row, col + 1, everywhere)
    west = lookup(row, col - 1 + cols, everywhere)
    north_east = lookup(row + 1, col + 1, jnp.logical_not(top))
    north_west = lookup(row + 1, col - 1 + cols, jnp.logical_not(top))
    south_east = lookup(row - 1, col + 1, row >= 1)
    south_west = lookup(row - 1, col - 1 + cols, row >= 1)
    table = jnp.stack([north, south, east, west, north_east, north_west, south_east, south_west], axis=1).astype(jnp.int32)
    relabel = jax.random.permutation(jax.random.fold_in(key, 23), TILES).astype(jnp.int32)
    mapped = jnp.where(table >= 0, relabel[jnp.maximum(table, 0)], -1).astype(jnp.int32)
    new_table = jnp.zeros((TILES, 8), jnp.int32).at[relabel].set(mapped)
    new_flag = jnp.zeros((TILES,), jnp.int32).at[relabel].set(top.astype(jnp.int32))
    return (new_table, new_flag)


def draw_neighbours(key, part):
    return tile_layout(key)[0]


def draw_fold_flag(key, part):
    return tile_layout(key)[1]


def set_ends(drawn, stream_key, least, high):
    shape = drawn.shape
    index_at = [jax.random.randint(jax.random.fold_in(stream_key, axis), (), 0, shape[axis]) for axis in range(len(shape))]
    drawn = drawn.at[tuple(index_at)].set(least)
    longest = shape.index(max(shape))
    index_at[longest] = (index_at[longest] + 1) % shape[longest]
    return drawn.at[tuple(index_at)].set(high)


def block_levels(stream_key, dims, pieces, least, top_value):
    def one(dim, blocks):
        heights = jax.random.uniform(jax.random.fold_in(jax.random.fold_in(stream_key, 6), dim), (blocks,), jnp.float32, least / len(pieces), top_value / len(pieces))
        return jnp.repeat(jnp.exp(heights), dims[dim] // blocks).reshape((-1,) + (1,) * (len(dims) - dim - 1))

    factor_of = one(*pieces[0])
    for cut in pieces[1:]:
        factor_of = factor_of * one(*cut)
    return factor_of


def normal_values(stream_key, shape, spread, bound, cuts=(), held_as=jnp.bfloat16):
    factor_of = block_levels(stream_key, shape, cuts, -0.22, 0.18) if cuts else 1.0
    array = jax.random.normal(stream_key, shape, jnp.float32) * spread * factor_of
    return jnp.minimum(jnp.maximum(array, -bound), bound).astype(held_as)


def setup_inputs(seed: int = 0) -> dict:
    splits = jax.random.split(jax.random.key(seed), 8)
    return {
        "input_states": normal_values(splits[0], (N_DP, TILES, CH, SIDE * SIDE), 1.0, 6.0, ((0, 4), (1, 8))),
        "loss_sensitivity": normal_values(splits[1], (N_DP, TILES, CH, SIDE * SIDE), 1.0, 6.0, ((0, 4), (1, 8))),
        "ocean": set_ends((jax.random.randint(splits[2], (TILES, SIDE * SIDE), 0, 8) < 7).astype(jnp.int32), jax.random.fold_in(splits[2], 1), 0, 1),
        "neighbours": draw_neighbours(jax.random.fold_in(splits[7], 71), 0),
        "fold_flag": draw_fold_flag(jax.random.fold_in(splits[7], 71), 0),
        "w_first": normal_values(splits[5], (9, CH, CH), (9 * CH) ** -0.5, 0.125),
        "w_second": normal_values(splits[6], (9, CH, CH), (9 * CH) ** -0.5, 0.125),
    }


SQRT_TWO_PI = 0.7978845608028654
CUBIC = 0.044715

def gelu_pair(a):
    inner = SQRT_TWO_PI * (a + CUBIC * a * a * a)
    tangent = jnp.tanh(inner)
    value = 0.5 * a * (1.0 + tangent)
    slope = 0.5 * (1.0 + tangent) + 0.5 * a * (1.0 - tangent * tangent) * SQRT_TWO_PI * (1.0 + 3.0 * CUBIC * a * a)
    return (value, slope)

def pad_all(field, neighbours, fold_flag):
    patch_extent = field.shape[2]
    row_low = field[:, :, 0, :]
    row_high = field[:, :, patch_extent - 1, :]
    col_low = field[:, :, :, 0]
    col_high = field[:, :, :, patch_extent - 1]

    def pick(strip, k):
        index = neighbours[:, k]
        valid = (index >= 0).astype(jnp.float32)
        return strip[jnp.maximum(index, 0)] * valid[:, None, None]
    north = jnp.where((fold_flag == 1)[:, None, None], pick(row_high, 0)[:, :, ::-1], pick(row_low, 0))
    south = pick(row_high, 1)
    east = pick(col_low, 2)
    west = pick(col_high, 3)
    north_east = pick(row_low, 4)[:, :, 0:1]
    north_west = pick(row_low, 5)[:, :, patch_extent - 1:patch_extent]
    south_east = pick(row_high, 6)[:, :, 0:1]
    south_west = pick(row_high, 7)[:, :, patch_extent - 1:patch_extent]
    middle = jnp.concatenate([west[..., None], field, east[..., None]], axis=3)
    bottom = jnp.concatenate([south_west, south, south_east], axis=2)[:, :, None, :]
    top = jnp.concatenate([north_west, north, north_east], axis=2)[:, :, None, :]
    return jnp.concatenate([bottom, middle, top], axis=2)

def conv_ref(padded, weights):
    patch_extent = padded.shape[2] - 2
    total = jnp.zeros((padded.shape[0], weights.shape[1], patch_extent, patch_extent), jnp.float32)
    for k in range(9):
        shift_r = k // 3 - 1
        shift_c = k % 3 - 1
        window = padded[:, :, 1 + shift_r:1 + shift_r + patch_extent, 1 + shift_c:1 + shift_c + patch_extent]
        total = total + jnp.einsum('oi,tirc->torc', weights[k], window, precision=lax.Precision.HIGHEST)
    return total

def reference(input_states, loss_sensitivity, ocean, neighbours, fold_flag, w_first, w_second):
    patch_total = input_states.shape[1]
    feature_depth = input_states.shape[2]
    patch_extent = SIDE
    water_indicator = ocean.astype(jnp.float32).reshape(patch_total, 1, patch_extent, patch_extent)
    first = w_first.astype(jnp.float32)
    second = w_second.astype(jnp.float32)

    def solitary_bundle(pair):
        tiles, grads = pair
        inputs = tiles.astype(jnp.float32).reshape(patch_total, feature_depth, patch_extent, patch_extent)
        in_padded = pad_all(inputs, neighbours, fold_flag)
        pre_first = conv_ref(in_padded, first)
        value, slope = gelu_pair(pre_first)
        hidden = (value * water_indicator).astype(jnp.bfloat16)
        hidden = lax.optimization_barrier(hidden).astype(jnp.float32)

        def layer_two(weights, field):
            return conv_ref(pad_all(field, neighbours, fold_flag), weights)
        latter_linear_response, pull_two = jax.vjp(layer_two, second, hidden)
        prediction = (latter_linear_response * water_indicator).astype(jnp.bfloat16).reshape(patch_total, feature_depth, patch_extent * patch_extent)
        masked = grads.astype(jnp.float32).reshape(patch_total, feature_depth, patch_extent, patch_extent) * water_indicator
        latter_kernel_slope, back = pull_two(masked)
        pre_grad = (back * water_indicator * slope).astype(jnp.bfloat16)
        pre_grad = lax.optimization_barrier(pre_grad).astype(jnp.float32)
        _, pull_one = jax.vjp(lambda weights: conv_ref(in_padded, weights), first)
        earlier_kernel_slope, = pull_one(pre_grad)
        return (prediction, earlier_kernel_slope, latter_kernel_slope)
    prediction, earlier_kernel_slope, latter_kernel_slope = lax.map(solitary_bundle, (input_states, loss_sensitivity))
    return (prediction, lax.optimization_barrier(jnp.sum(earlier_kernel_slope, axis=0)), lax.optimization_barrier(jnp.sum(latter_kernel_slope, axis=0)))
```

```python
import functools

import jax
import jax.numpy as jnp
from jax import lax
from jax.experimental import pallas as pl
from jax.experimental.pallas import tpu as pltpu
from jax.sharding import PartitionSpec as P

SIDE = 32
CELLS = SIDE * SIDE
EXT = CELLS + 2 * SIDE
SQRT_TWO_PI = 0.7978845608028654
CUBIC = 0.044715
F32 = jnp.float32
BF16 = jnp.bfloat16
NN = (((1,), (0,)), ((), ()))
NT = (((1,), (1,)), ((), ()))


def matmul(a, b, dims=NN):
    return lax.dot_general(a, b, dims, preferred_element_type=F32)


def gelu_pair(a):
    inner = SQRT_TWO_PI * (a + CUBIC * a * a * a)
    tangent = jnp.tanh(inner)
    value = 0.5 * a * (1.0 + tangent)
    slope = 0.5 * (1.0 + tangent) + 0.5 * a * (1.0 - tangent * tangent) * SQRT_TWO_PI * (
        1.0 + 3.0 * CUBIC * a * a
    )
    return (value, slope)


def each(count, step):
    if count <= 8:
        for q in range(count):
            step(q)
    else:
        lax.fori_loop(0, count, lambda q, c: (step(q), c)[1], 0)


def kernel(
    n_space, rows,
    x_ref, g_ref, ocean_ref, nb_ref, flag_ref, w1_ref, w2_ref,
    pred_ref, out1_ref, out2_ref,
    gath0, gath1, gath2, pads, hidden_ref, slope_ref, gt_ref, mask_ref, acc, stage, land, res,
    near_send, far_send, strip_recv, red_send, red_recv,
):
    depth = x_ref.shape[0]
    half_n = n_space // 2
    me = lax.axis_index("space")
    dp = lax.axis_index("dp")
    y = me % 2
    z = me // 2
    core = dp % 2
    x = dp // 2
    mate = z * 2 + (1 - y)
    core_mate = x * 2 + (1 - core)
    x_mate = (1 - x) * 2 + core
    mesh_id = pl.DeviceIdType.MESH
    gath = (gath0, gath1, gath2)

    def peer(q):
        return (z + q) % half_n

    def source(q):
        return (z + half_n - q) % half_n

    barrier = pltpu.get_barrier_semaphore()

    def greet(space_to, dp_to):
        pl.semaphore_signal(barrier, inc=1, device_id=(space_to, dp_to), device_id_type=mesh_id)

    each(half_n - 1, lambda q: greet(peer(q + 1) * 2 + y, dp))
    greet(mate, dp)
    greet(me, core_mate)
    greet(me, x_mate)

    def near_copy(f, q):
        return pltpu.make_async_remote_copy(
            src_ref=gath[f].at[me], dst_ref=gath[f].at[me],
            send_sem=near_send.at[f, q], recv_sem=strip_recv.at[f, me],
            device_id=(peer(q) * 2 + y, dp), device_id_type=mesh_id)

    def far_copy(f, q):
        slot = source(q) * 2 + y
        return pltpu.make_async_remote_copy(
            src_ref=gath[f].at[slot], dst_ref=gath[f].at[slot],
            send_sem=far_send.at[f, q], recv_sem=strip_recv.at[f, slot],
            device_id=(mate, dp), device_id_type=mesh_id)

    def arrived(f, slot):
        pltpu.make_async_remote_copy(
            src_ref=gath[f].at[slot], dst_ref=gath[f].at[slot],
            send_sem=near_send.at[f, 0], recv_sem=strip_recv.at[f, slot],
            device_id=(mate, dp), device_id_type=mesh_id).wait_recv()

    def send_own(f):
        each(half_n - 1, lambda q: near_copy(f, q + 1).start())
        far_copy(f, 0).start()

    def forward(f):
        def step(q):
            arrived(f, source(q + 1) * 2 + y)
            far_copy(f, q + 1).start()
        each(half_n - 1, step)

    def collect(f):
        each(half_n, lambda q: arrived(f, source(q) * 2 + (1 - y)))

    def sent(f):
        def step(q):
            near_copy(f, q + 1).wait_send()
        each(half_n - 1, step)
        each(half_n, lambda q: far_copy(f, q).wait_send())

    j = lax.broadcasted_iota(jnp.int32, (4 * SIDE, CELLS), 0)
    c = lax.broadcasted_iota(jnp.int32, (4 * SIDE, CELLS), 1)
    cell = jnp.where(
        j < SIDE, j,
        jnp.where(j < 2 * SIDE, j + (CELLS - 2 * SIDE),
                  jnp.where(j < 3 * SIDE, (j - 2 * SIDE) * SIDE, (j - 3 * SIDE) * SIDE + SIDE - 1)))
    pick = (c == cell).astype(F32).astype(BF16)

    ocean_row = ocean_ref[...].astype(F32)
    gt = (g_ref[...].astype(F32) * ocean_row).astype(BF16)
    gt_ref[...] = gt
    gath0[me] = matmul(pick, x_ref[...], NT).astype(BF16)
    gath1[me] = matmul(pick, gt, NT).astype(BF16)
    pl.semaphore_wait(barrier, half_n + 2)
    send_own(0)
    send_own(1)

    ocean_t = jnp.transpose(jnp.broadcast_to(ocean_row, (128, CELLS)))
    mask_ref[...] = jnp.concatenate([ocean_t, ocean_t], axis=1)[:, :depth]

    fold = flag_ref[0]
    ext_row = lax.broadcasted_iota(jnp.int32, (EXT, 3 * SIDE), 0)
    col = lax.broadcasted_iota(jnp.int32, (EXT, 3 * SIDE), 1)
    line = ext_row // SIDE
    spot = ext_row % SIDE
    last = SIDE + 1
    east_col = jnp.where(line == 0, SIDE, jnp.where(line == last, 2 * SIDE, line - 1))
    west_col = jnp.where(line == 0, 2 * SIDE - 1, jnp.where(line == last, 3 * SIDE - 1, line - 1))
    east_put = ((spot == SIDE - 1) & (col == east_col)).astype(F32).astype(BF16)
    west_put = ((spot == 0) & (col == west_col)).astype(F32).astype(BF16)
    nr = lax.broadcasted_iota(jnp.int32, (SIDE, 2 * SIDE), 0)
    nc = lax.broadcasted_iota(jnp.int32, (SIDE, 2 * SIDE), 1)
    north_put = (nc == jnp.where(fold == 1, 2 * SIDE - 1 - nr, nr)).astype(F32).astype(BF16)
    wide = lax.broadcasted_iota(jnp.int32, (EXT, depth), 0) % SIDE

    def build(f, field):
        def block(k, part, count=1):
            index = nb_ref[0, k]
            valid = (index >= 0).astype(F32)
            got = gath[f][jnp.maximum(index, 0), part * SIDE:(part + count) * SIDE, :]
            return got.astype(F32) * valid

        north = matmul(north_put, block(0, 0, 2).astype(BF16))
        south = block(1, 1)
        ext = jnp.concatenate([south, field, north], axis=0)
        east = jnp.concatenate([block(2, 2), block(6, 1), block(4, 0)], axis=0).astype(BF16)
        west = jnp.concatenate([block(3, 3), block(7, 1), block(5, 0)], axis=0).astype(BF16)
        pads[f, 1] = ext.astype(BF16)
        plus = jnp.where(wide == SIDE - 1, 0.0, pltpu.roll(ext, EXT - 1, 0))
        pads[f, 2] = (plus + matmul(east_put, east)).astype(BF16)
        minus = jnp.where(wide == 0, 0.0, pltpu.roll(ext, 1, 0))
        pads[f, 0] = (minus + matmul(west_put, west)).astype(BF16)

    def window(f, dr, dc):
        start = SIDE * (dr + 1)
        return pads[f, dc + 1, start:start + CELLS, :]

    def conv(f, w_ref):
        total = None
        for k in range(9):
            term = matmul(window(f, k // 3 - 1, k % 3 - 1), w_ref[k], NT)
            total = term if total is None else total + term
        return total

    def weight_grad(s, grads, f):
        for k in range(9):
            acc[s, k * depth:(k + 1) * depth, :] = matmul(grads, window(f, k // 3 - 1, k % 3 - 1))

    ways = (
        ((core, (me, core_mate)), (x, (me, x_mate)), (y, (mate, dp))),
        ((core, (me, core_mate)), (y, (mate, dp)), (x, (me, x_mate))),
    )
    offsets = []
    for s in range(2):
        off = 0
        marks = []
        for t, (bit, _) in enumerate(ways[s]):
            size = rows >> (t + 1)
            marks.append((off + bit * size, off + (1 - bit) * size))
            off = off + bit * size
        offsets.append(marks)
    piece = rows // (8 * half_n)

    def span(start, size):
        return pl.ds(pl.multiple_of(start, 16), size)

    def halve_copy(s, t):
        size = rows >> (t + 1)
        return pltpu.make_async_remote_copy(
            src_ref=stage.at[s, span(offsets[s][t][1], size)],
            dst_ref=land.at[s, pl.ds(rows - 2 * size, size)],
            send_sem=red_send.at[s, t], recv_sem=red_recv.at[s, t],
            device_id=ways[s][t][1], device_id_type=mesh_id)

    def halve_start(s, t):
        size = rows >> (t + 1)
        away = span(offsets[s][t][1], size)
        stage[s, away] = acc[s, away].astype(BF16)
        halve_copy(s, t).start()

    def halve_end(s, t):
        size = rows >> (t + 1)
        halve_copy(s, t).wait_recv()
        keep = span(offsets[s][t][0], size)
        acc[s, keep] = acc[s, keep] + land[s, pl.ds(rows - 2 * size, size)].astype(F32)

    base = rows - rows // 8

    def z_copy(s, q):
        off = offsets[s][2][0]
        return pltpu.make_async_remote_copy(
            src_ref=stage.at[s, span(off + peer(q) * piece, piece)],
            dst_ref=land.at[s, span(base + z * piece, piece)],
            send_sem=red_send.at[s, 6 + q], recv_sem=red_recv.at[s, 6 + q],
            device_id=(peer(q) * 2 + y, dp), device_id_type=mesh_id)

    def z_start(s):
        whole = span(offsets[s][2][0], rows // 8)
        stage[s, whole] = acc[s, whole].astype(BF16)
        each(half_n - 1, lambda q: z_copy(s, q + 1).start())

    def z_end(s):
        mine = span(offsets[s][2][0] + z * piece, piece)

        def step(q):
            z_copy(s, q + 1).wait_recv()
            got = land[s, span(base + source(q + 1) * piece, piece)]
            acc[s, mine] = acc[s, mine] + got.astype(F32)
        each(half_n - 1, step)
        res[s, mine] = acc[s, mine].astype(BF16)

    def zg_copy(s, q):
        mine = span(offsets[s][2][0] + z * piece, piece)
        return pltpu.make_async_remote_copy(
            src_ref=res.at[s, mine], dst_ref=res.at[s, mine],
            send_sem=red_send.at[s, 6 + half_n + q], recv_sem=red_recv.at[s, 6 + half_n + q],
            device_id=(peer(q) * 2 + y, dp), device_id_type=mesh_id)

    def grow_copy(s, t):
        have = span(offsets[s][t][0], rows >> (t + 1))
        return pltpu.make_async_remote_copy(
            src_ref=res.at[s, have], dst_ref=res.at[s, have],
            send_sem=red_send.at[s, 3 + t], recv_sem=red_recv.at[s, 3 + t],
            device_id=ways[s][t][1], device_id_type=mesh_id)

    for s in range(2):
        acc[s, 9 * depth:] = jnp.zeros((rows - 9 * depth, depth), F32)
    forward(0)
    forward(1)
    field_x = jnp.transpose(x_ref[...].astype(F32))
    collect(0)
    build(0, field_x)
    value, slope = gelu_pair(conv(0, w1_ref))
    hidden = (value * mask_ref[...]).astype(BF16)
    hidden_ref[...] = hidden
    slope_ref[...] = slope * mask_ref[...]
    gath2[me] = matmul(pick, hidden).astype(BF16)
    send_own(2)

    field_g = jnp.transpose(gt_ref[...].astype(F32))
    collect(1)
    build(1, field_g)
    forward(2)
    back = None
    edge = None
    for k in (3, 4, 5, 6, 7, 8):
        term = matmul(window(1, 1 - k // 3, 1 - k % 3), w2_ref[k])
        back = term if back is None else back + term
    inner = None
    for k in range(3):
        dc = 1 - k % 3
        term = matmul(pads[1, dc + 1, 2 * SIDE:EXT - SIDE, :], w2_ref[k])
        inner = term if inner is None else inner + term
        across = jnp.where(fold == 1, w2_ref[8 - k].astype(F32), w2_ref[k].astype(F32)).astype(BF16)
        term = matmul(pads[1, dc + 1, EXT - SIDE:EXT, :], across)
        edge = term if edge is None else edge + term
    back = back + jnp.concatenate([inner, edge], axis=0)
    pre_grad = back * slope_ref[...]
    weight_grad(0, jnp.transpose(pre_grad).astype(BF16), 0)
    halve_start(0, 0)

    collect(2)
    build(2, hidden_ref[...].astype(F32))
    weight_grad(1, gt_ref[...], 2)
    halve_start(1, 0)
    halve_end(0, 0)
    halve_start(0, 1)
    forecast = conv(2, w2_ref) * mask_ref[...]
    pred_ref[...] = jnp.transpose(forecast).astype(BF16)
    halve_end(1, 0)
    halve_start(1, 1)
    halve_end(0, 1)
    halve_start(0, 2)
    halve_end(1, 1)
    halve_start(1, 2)
    halve_end(0, 2)
    z_start(0)
    halve_end(1, 2)
    z_start(1)
    for s in range(2):
        z_end(s)
        each(half_n - 1, lambda q: zg_copy(s, q + 1).start())
    for t in (2, 1, 0):
        for s in range(2):
            if t == 2:
                each(half_n - 1, lambda q: zg_copy(s, q + 1).wait_recv())
            else:
                grow_copy(s, t + 1).wait_recv()
            grow_copy(s, t).start()
    out_rows = out1_ref.shape[0]
    for s, out in enumerate((out1_ref, out2_ref)):
        grow_copy(s, 0).wait_recv()
        out[...] = res[s, :out_rows]
    for f in range(3):
        sent(f)
    for s in range(2):
        for t in range(3):
            halve_copy(s, t).wait_send()
            grow_copy(s, t).wait_send()

        def done(q):
            z_copy(s, q + 1).wait_send()
            zg_copy(s, q + 1).wait_send()
        each(half_n - 1, done)


def body(n_space, input_states, loss_sensitivity, ocean, neighbours, fold_flag, w_first, w_second):
    depth = input_states.shape[2]
    half_n = n_space // 2
    unit = 8 * half_n * 16
    used = 9 * depth
    rows = -(-used // unit) * unit
    vmem = pl.BlockSpec(memory_space=pltpu.VMEM)
    smem = pl.BlockSpec(memory_space=pltpu.SMEM)
    prediction, first, second = pl.pallas_call(
        functools.partial(kernel, n_space, rows),
        out_shape=(
            jax.ShapeDtypeStruct((depth, CELLS), BF16),
            jax.ShapeDtypeStruct((used, depth), BF16),
            jax.ShapeDtypeStruct((used, depth), BF16),
        ),
        in_specs=[vmem, vmem, vmem, smem, smem, vmem, vmem],
        out_specs=(vmem, vmem, vmem),
        scratch_shapes=[
            pltpu.VMEM((n_space, 4 * SIDE, depth), BF16),
            pltpu.VMEM((n_space, 4 * SIDE, depth), BF16),
            pltpu.VMEM((n_space, 4 * SIDE, depth), BF16),
            pltpu.VMEM((3, 3, EXT, depth), BF16),
            pltpu.VMEM((CELLS, depth), BF16),
            pltpu.VMEM((CELLS, depth), F32),
            pltpu.VMEM((depth, CELLS), BF16),
            pltpu.VMEM((CELLS, depth), F32),
            pltpu.VMEM((2, rows, depth), F32),
            pltpu.VMEM((2, rows, depth), BF16),
            pltpu.VMEM((2, rows, depth), BF16),
            pltpu.VMEM((2, rows, depth), BF16),
            pltpu.SemaphoreType.DMA((3, half_n)),
            pltpu.SemaphoreType.DMA((3, half_n)),
            pltpu.SemaphoreType.DMA((3, n_space)),
            pltpu.SemaphoreType.DMA((2, 6 + 2 * half_n)),
            pltpu.SemaphoreType.DMA((2, 6 + 2 * half_n)),
        ],
        compiler_params=pltpu.CompilerParams(
            collective_id=0, has_side_effects=True, vmem_limit_bytes=52 * 1024 * 1024),
    )(input_states[0, 0], loss_sensitivity[0, 0], ocean, neighbours, fold_flag, w_first, w_second)
    shape = (9, depth, depth)
    return (
        prediction[None, None],
        first.astype(F32).reshape(shape),
        second.astype(F32).reshape(shape),
    )


def solution(mesh):
    placed = (
        P("dp", "space", None, None),
        P("dp", "space", None, None),
        P("space", None),
        P("space", None),
        P("space"),
        P(),
        P(),
    )
    return jax.shard_map(
        functools.partial(body, mesh.shape["space"]),
        mesh=mesh,
        in_specs=placed,
        out_specs=(P("dp", "space", None, None), P(), P()),
        check_vma=False,
    )
```

```python
import functools

import jax
import jax.numpy as jnp
from jax import lax
from jax.experimental import pallas as pl
from jax.experimental.pallas import tpu as pltpu
from jax.sharding import PartitionSpec as P

SIDE = 32
CELLS = SIDE * SIDE
EXT = CELLS + 2 * SIDE
LANES = 128
SQRT_TWO_PI = 0.7978845608028654
CUBIC = 0.044715
F32 = jnp.float32
BF16 = jnp.bfloat16
NN = (((1,), (0,)), ((), ()))
NT = (((1,), (1,)), ((), ()))


def matmul(a, b, dims=NN):
    return lax.dot_general(a, b, dims, preferred_element_type=F32)


def gelu_pair(a):
    inner = SQRT_TWO_PI * (a + CUBIC * a * a * a)
    tangent = jnp.tanh(inner)
    value = 0.5 * a * (1.0 + tangent)
    slope = 0.5 * (1.0 + tangent) + 0.5 * a * (1.0 - tangent * tangent) * SQRT_TWO_PI * (
        1.0 + 3.0 * CUBIC * a * a
    )
    return (value, slope)


def each(count, step):
    if count <= 8:
        for q in range(count):
            step(q)
    else:
        lax.fori_loop(0, count, lambda q, c: (step(q), c)[1], 0)


def kernel(
    n_space, rows, tiles,
    x_ref, g_ref, ocean_ref, nb_ref, flag_ref, w1_ref, w2_ref,
    pred_ref, out1_ref, out2_ref,
    gath0, gath1, gath2, pads, hidden_ref, slope_ref, gt_ref, mask_ref, acc, stage, land, res,
    near_send, far_send, strip_recv, red_send, red_recv,
):
    depth = x_ref.shape[0]
    half_n = n_space // 2
    used = 3 * depth * tiles
    me = lax.axis_index("space")
    dp = lax.axis_index("dp")
    y = me % 2
    z = me // 2
    core = dp % 2
    x = dp // 2
    mate = z * 2 + (1 - y)
    core_mate = x * 2 + (1 - core)
    x_mate = (1 - x) * 2 + core
    mesh_id = pl.DeviceIdType.MESH
    gath = (gath0, gath1, gath2)

    def peer(q):
        return (z + q) % half_n

    def source(q):
        return (z + half_n - q) % half_n

    barrier = pltpu.get_barrier_semaphore()

    def greet(space_to, dp_to):
        pl.semaphore_signal(barrier, inc=1, device_id=(space_to, dp_to), device_id_type=mesh_id)

    each(half_n - 1, lambda q: greet(peer(q + 1) * 2 + y, dp))
    greet(mate, dp)
    greet(me, core_mate)
    greet(me, x_mate)

    def near_copy(f, q):
        return pltpu.make_async_remote_copy(
            src_ref=gath[f].at[me], dst_ref=gath[f].at[me],
            send_sem=near_send.at[f, q], recv_sem=strip_recv.at[f, me],
            device_id=(peer(q) * 2 + y, dp), device_id_type=mesh_id)

    def far_copy(f, q):
        slot = source(q) * 2 + y
        return pltpu.make_async_remote_copy(
            src_ref=gath[f].at[slot], dst_ref=gath[f].at[slot],
            send_sem=far_send.at[f, q], recv_sem=strip_recv.at[f, slot],
            device_id=(mate, dp), device_id_type=mesh_id)

    def arrived(f, slot):
        pltpu.make_async_remote_copy(
            src_ref=gath[f].at[slot], dst_ref=gath[f].at[slot],
            send_sem=near_send.at[f, 0], recv_sem=strip_recv.at[f, slot],
            device_id=(mate, dp), device_id_type=mesh_id).wait_recv()

    def send_own(f):
        each(half_n - 1, lambda q: near_copy(f, q + 1).start())
        far_copy(f, 0).start()

    def forward(f):
        def step(q):
            arrived(f, source(q + 1) * 2 + y)
            far_copy(f, q + 1).start()
        each(half_n - 1, step)

    def collect(f):
        each(half_n, lambda q: arrived(f, source(q) * 2 + (1 - y)))

    def sent(f):
        def step(q):
            near_copy(f, q + 1).wait_send()
        each(half_n - 1, step)
        each(half_n, lambda q: far_copy(f, q).wait_send())

    j = lax.broadcasted_iota(jnp.int32, (4 * SIDE, CELLS), 0)
    c = lax.broadcasted_iota(jnp.int32, (4 * SIDE, CELLS), 1)
    cell = jnp.where(
        j < SIDE, j,
        jnp.where(j < 2 * SIDE, j + (CELLS - 2 * SIDE),
                  jnp.where(j < 3 * SIDE, (j - 2 * SIDE) * SIDE, (j - 3 * SIDE) * SIDE + SIDE - 1)))
    pick = (c == cell).astype(F32).astype(BF16)

    ocean_row = ocean_ref[...].astype(F32)
    gt = (g_ref[...].astype(F32) * ocean_row).astype(BF16)
    gt_ref[...] = gt
    gath0[me] = matmul(pick, x_ref[...], NT).astype(BF16)
    gath1[me] = matmul(pick, gt, NT).astype(BF16)
    pl.semaphore_wait(barrier, half_n + 2)
    send_own(0)
    send_own(1)

    ocean_t = jnp.transpose(jnp.broadcast_to(ocean_row, (128, CELLS)))
    mask_ref[...] = jnp.concatenate([ocean_t, ocean_t], axis=1)[:, :depth]

    fold = flag_ref[0]
    ext_row = lax.broadcasted_iota(jnp.int32, (EXT, 3 * SIDE), 0)
    col = lax.broadcasted_iota(jnp.int32, (EXT, 3 * SIDE), 1)
    line = ext_row // SIDE
    spot = ext_row % SIDE
    last = SIDE + 1
    east_col = jnp.where(line == 0, SIDE, jnp.where(line == last, 2 * SIDE, line - 1))
    west_col = jnp.where(line == 0, 2 * SIDE - 1, jnp.where(line == last, 3 * SIDE - 1, line - 1))
    east_put = ((spot == SIDE - 1) & (col == east_col)).astype(F32).astype(BF16)
    west_put = ((spot == 0) & (col == west_col)).astype(F32).astype(BF16)
    nr = lax.broadcasted_iota(jnp.int32, (SIDE, 2 * SIDE), 0)
    nc = lax.broadcasted_iota(jnp.int32, (SIDE, 2 * SIDE), 1)
    north_put = (nc == jnp.where(fold == 1, 2 * SIDE - 1 - nr, nr)).astype(F32).astype(BF16)
    wide = lax.broadcasted_iota(jnp.int32, (EXT, depth), 0) % SIDE

    def build(f, field):
        def block(k, part, count=1):
            index = nb_ref[0, k]
            valid = (index >= 0).astype(F32)
            got = gath[f][jnp.maximum(index, 0), part * SIDE:(part + count) * SIDE, :]
            return got.astype(F32) * valid

        north = matmul(north_put, block(0, 0, 2).astype(BF16))
        south = block(1, 1)
        ext = jnp.concatenate([south, field, north], axis=0)
        east = jnp.concatenate([block(2, 2), block(6, 1), block(4, 0)], axis=0).astype(BF16)
        west = jnp.concatenate([block(3, 3), block(7, 1), block(5, 0)], axis=0).astype(BF16)
        pads[f, 1] = ext.astype(BF16)
        plus = jnp.where(wide == SIDE - 1, 0.0, pltpu.roll(ext, EXT - 1, 0))
        pads[f, 2] = (plus + matmul(east_put, east)).astype(BF16)
        minus = jnp.where(wide == 0, 0.0, pltpu.roll(ext, 1, 0))
        pads[f, 0] = (minus + matmul(west_put, west)).astype(BF16)

    def window(f, dr, dc):
        start = SIDE * (dr + 1)
        return pads[f, dc + 1, start:start + CELLS, :]

    def conv(f, w_ref):
        total = None
        for k in range(9):
            term = matmul(window(f, k // 3 - 1, k % 3 - 1), w_ref[k], NT)
            total = term if total is None else total + term
        return total

    def weight_grad(s, grads, f):
        for dr in range(3):
            parts = [matmul(grads, window(f, dr - 1, dc - 1)) for dc in range(3)]
            spare = jnp.zeros((depth, LANES * tiles - 3 * depth), F32)
            wide = jnp.concatenate(parts + [spare], axis=1)
            for t in range(tiles):
                start = (3 * t + dr) * depth
                acc[s, start:start + depth, :] = wide[:, LANES * t:LANES * (t + 1)]

    by_core = (core, (me, core_mate))
    by_x = (x, (me, x_mate))
    by_y = (y, (mate, dp))
    ways = ((by_core, by_x, by_y), (by_core, by_y, by_x)) * 2
    part = rows // 2
    offsets = []
    for u in range(4):
        off = (u % 2) * part
        marks = []
        for t, (bit, _) in enumerate(ways[u]):
            size = part >> (t + 1)
            marks.append((off + bit * size, off + (1 - bit) * size))
            off = off + bit * size
        offsets.append(marks)
    piece = part // (8 * half_n)

    def span(start, size):
        return pl.ds(pl.multiple_of(start, 16), size)

    def landing(u, t):
        size = part >> (t + 1)
        return pl.ds((u % 2) * part + part - 2 * size, size)

    def halve_copy(u, t):
        return pltpu.make_async_remote_copy(
            src_ref=stage.at[u // 2, span(offsets[u][t][1], part >> (t + 1))],
            dst_ref=land.at[u // 2, landing(u, t)],
            send_sem=red_send.at[u, t], recv_sem=red_recv.at[u, t],
            device_id=ways[u][t][1], device_id_type=mesh_id)

    def halve_start(u, t):
        away = span(offsets[u][t][1], part >> (t + 1))
        stage[u // 2, away] = acc[u // 2, away].astype(BF16)
        halve_copy(u, t).start()

    def halve_end(u, t):
        halve_copy(u, t).wait_recv()
        keep = span(offsets[u][t][0], part >> (t + 1))
        acc[u // 2, keep] = acc[u // 2, keep] + land[u // 2, landing(u, t)].astype(F32)

    def z_land(u, zp):
        return span((u % 2) * part + part - part // 8 + zp * piece, piece)

    def z_copy(u, q):
        off = offsets[u][2][0]
        return pltpu.make_async_remote_copy(
            src_ref=stage.at[u // 2, span(off + peer(q) * piece, piece)],
            dst_ref=land.at[u // 2, z_land(u, z)],
            send_sem=red_send.at[u, 6 + q], recv_sem=red_recv.at[u, 6 + q],
            device_id=(peer(q) * 2 + y, dp), device_id_type=mesh_id)

    def z_start(u):
        whole = span(offsets[u][2][0], part // 8)
        stage[u // 2, whole] = acc[u // 2, whole].astype(BF16)
        each(half_n - 1, lambda q: z_copy(u, q + 1).start())

    def z_end(u):
        mine = span(offsets[u][2][0] + z * piece, piece)

        def step(q):
            z_copy(u, q + 1).wait_recv()
            got = land[u // 2, z_land(u, source(q + 1))]
            acc[u // 2, mine] = acc[u // 2, mine] + got.astype(F32)
        each(half_n - 1, step)
        res[u // 2, mine] = acc[u // 2, mine].astype(BF16)

    def zg_copy(u, q):
        mine = span(offsets[u][2][0] + z * piece, piece)
        return pltpu.make_async_remote_copy(
            src_ref=res.at[u // 2, mine], dst_ref=res.at[u // 2, mine],
            send_sem=red_send.at[u, 6 + half_n + q], recv_sem=red_recv.at[u, 6 + half_n + q],
            device_id=(peer(q) * 2 + y, dp), device_id_type=mesh_id)

    def grow_copy(u, t):
        have = span(offsets[u][t][0], part >> (t + 1))
        return pltpu.make_async_remote_copy(
            src_ref=res.at[u // 2, have], dst_ref=res.at[u // 2, have],
            send_sem=red_send.at[u, 3 + t], recv_sem=red_recv.at[u, 3 + t],
            device_id=ways[u][t][1], device_id_type=mesh_id)

    for s in range(2):
        acc[s, used:] = jnp.zeros((rows - used, LANES), F32)
    forward(0)
    forward(1)
    field_x = jnp.transpose(x_ref[...].astype(F32))
    collect(0)
    build(0, field_x)
    value, slope = gelu_pair(conv(0, w1_ref))
    hidden = (value * mask_ref[...]).astype(BF16)
    hidden_ref[...] = hidden
    slope_ref[...] = slope * mask_ref[...]
    gath2[me] = matmul(pick, hidden).astype(BF16)
    send_own(2)

    field_g = jnp.transpose(gt_ref[...].astype(F32))
    collect(1)
    build(1, field_g)
    forward(2)
    back = None
    edge = None
    for k in (3, 4, 5, 6, 7, 8):
        term = matmul(window(1, 1 - k // 3, 1 - k % 3), w2_ref[k])
        back = term if back is None else back + term
    inner = None
    for k in range(3):
        dc = 1 - k % 3
        term = matmul(pads[1, dc + 1, 2 * SIDE:EXT - SIDE, :], w2_ref[k])
        inner = term if inner is None else inner + term
        across = jnp.where(fold == 1, w2_ref[8 - k].astype(F32), w2_ref[k].astype(F32)).astype(BF16)
        term = matmul(pads[1, dc + 1, EXT - SIDE:EXT, :], across)
        edge = term if edge is None else edge + term
    back = back + jnp.concatenate([inner, edge], axis=0)
    pre_grad = back * slope_ref[...]
    weight_grad(0, jnp.transpose(pre_grad).astype(BF16), 0)
    halve_start(0, 0)
    halve_start(1, 0)

    collect(2)
    build(2, hidden_ref[...].astype(F32))
    for u in (0, 1):
        halve_end(u, 0)
        halve_start(u, 1)
    weight_grad(1, gt_ref[...], 2)
    halve_start(2, 0)
    halve_start(3, 0)
    for u in (0, 1):
        halve_end(u, 1)
        halve_start(u, 2)
    forecast = conv(2, w2_ref) * mask_ref[...]
    for u in (2, 3):
        halve_end(u, 0)
        halve_start(u, 1)
    for u in (0, 1):
        halve_end(u, 2)
        z_start(u)
    pred_ref[...] = jnp.transpose(forecast).astype(BF16)
    for u in (2, 3):
        halve_end(u, 1)
        halve_start(u, 2)

    def finish(u):
        z_end(u)
        each(half_n - 1, lambda q: zg_copy(u, q + 1).start())

    def grow(u, t):
        if t == 2:
            each(half_n - 1, lambda q: zg_copy(u, q + 1).wait_recv())
        else:
            grow_copy(u, t + 1).wait_recv()
        grow_copy(u, t).start()

    def unpack(s, out):
        grow_copy(2 * s, 0).wait_recv()
        grow_copy(2 * s + 1, 0).wait_recv()
        total = res[s].astype(F32)
        for dr in range(3):
            starts = [(3 * t + dr) * depth for t in range(tiles)]
            wide = jnp.concatenate([total[r:r + depth] for r in starts], axis=1)
            for dc in range(3):
                out[3 * dr + dc] = wide[:, dc * depth:(dc + 1) * depth].astype(BF16)

    finish(0)
    finish(1)
    for u in (2, 3):
        halve_end(u, 2)
        z_start(u)
    grow(0, 2)
    grow(1, 2)
    finish(2)
    finish(3)
    grow(0, 1)
    grow(1, 1)
    grow(2, 2)
    grow(3, 2)
    grow(0, 0)
    grow(1, 0)
    grow(2, 1)
    grow(3, 1)
    unpack(0, out1_ref)
    grow(2, 0)
    grow(3, 0)
    unpack(1, out2_ref)
    for f in range(3):
        sent(f)
    for u in range(4):
        for t in range(3):
            halve_copy(u, t).wait_send()
            grow_copy(u, t).wait_send()

        def done(q):
            z_copy(u, q + 1).wait_send()
            zg_copy(u, q + 1).wait_send()
        each(half_n - 1, done)


def body(n_space, input_states, loss_sensitivity, ocean, neighbours, fold_flag, w_first, w_second):
    depth = input_states.shape[2]
    half_n = n_space // 2
    unit = 16 * half_n * 16
    tiles = -(-3 * depth // LANES)
    used = 3 * depth * tiles
    rows = -(-used // unit) * unit
    vmem = pl.BlockSpec(memory_space=pltpu.VMEM)
    smem = pl.BlockSpec(memory_space=pltpu.SMEM)
    prediction, first, second = pl.pallas_call(
        functools.partial(kernel, n_space, rows, tiles),
        out_shape=(
            jax.ShapeDtypeStruct((depth, CELLS), BF16),
            jax.ShapeDtypeStruct((9, depth, depth), BF16),
            jax.ShapeDtypeStruct((9, depth, depth), BF16),
        ),
        in_specs=[vmem, vmem, vmem, smem, smem, vmem, vmem],
        out_specs=(vmem, vmem, vmem),
        scratch_shapes=[
            pltpu.VMEM((n_space, 4 * SIDE, depth), BF16),
            pltpu.VMEM((n_space, 4 * SIDE, depth), BF16),
            pltpu.VMEM((n_space, 4 * SIDE, depth), BF16),
            pltpu.VMEM((3, 3, EXT, depth), BF16),
            pltpu.VMEM((CELLS, depth), BF16),
            pltpu.VMEM((CELLS, depth), F32),
            pltpu.VMEM((depth, CELLS), BF16),
            pltpu.VMEM((CELLS, depth), F32),
            pltpu.VMEM((2, rows, LANES), F32),
            pltpu.VMEM((2, rows, LANES), BF16),
            pltpu.VMEM((2, rows, LANES), BF16),
            pltpu.VMEM((2, rows, LANES), BF16),
            pltpu.SemaphoreType.DMA((3, half_n)),
            pltpu.SemaphoreType.DMA((3, half_n)),
            pltpu.SemaphoreType.DMA((3, n_space)),
            pltpu.SemaphoreType.DMA((4, 6 + 2 * half_n)),
            pltpu.SemaphoreType.DMA((4, 6 + 2 * half_n)),
        ],
        compiler_params=pltpu.CompilerParams(
            collective_id=0, has_side_effects=True, vmem_limit_bytes=(32 + n_space // 4) * 1024 * 1024),
    )(input_states[0, 0], loss_sensitivity[0, 0], ocean, neighbours, fold_flag, w_first, w_second)
    return (prediction[None, None], first.astype(F32), second.astype(F32))


def solution(mesh):
    placed = (
        P("dp", "space", None, None),
        P("dp", "space", None, None),
        P("space", None),
        P("space", None),
        P("space"),
        P(),
        P(),
    )
    return jax.shard_map(
        functools.partial(body, mesh.shape["space"]),
        mesh=mesh,
        in_specs=placed,
        out_specs=(P("dp", "space", None, None), P(), P()),
        check_vma=False,
    )
```

```python
import functools

import jax
import jax.numpy as jnp
from jax import lax
from jax.experimental import pallas as pl
from jax.experimental.pallas import tpu as pltpu
from jax.sharding import PartitionSpec as P

SIDE = 32
CELLS = SIDE * SIDE
EXT = CELLS + 2 * SIDE
LANES = 128
SQRT_TWO_PI = 0.7978845608028654
CUBIC = 0.044715
F32 = jnp.float32
BF16 = jnp.bfloat16
NN = (((1,), (0,)), ((), ()))
NT = (((1,), (1,)), ((), ()))


def matmul(a, b, dims=NN):
    return lax.dot_general(a, b, dims, preferred_element_type=F32)


def gelu_pair(a):
    inner = SQRT_TWO_PI * (a + CUBIC * a * a * a)
    tangent = jnp.tanh(inner)
    value = 0.5 * a * (1.0 + tangent)
    slope = 0.5 * (1.0 + tangent) + 0.5 * a * (1.0 - tangent * tangent) * SQRT_TWO_PI * (
        1.0 + 3.0 * CUBIC * a * a
    )
    return (value, slope)


def each(count, step):
    if count <= 8:
        for q in range(count):
            step(q)
    else:
        lax.fori_loop(0, count, lambda q, c: (step(q), c)[1], 0)


def kernel(
    n_space, rows, tiles,
    x_ref, g_ref, ocean_ref, nb_ref, flag_ref, w1_far, w2_far,
    pred_ref, out1_ref, out2_ref,
    gath0, gath1, gath2, pads, hidden_ref, slope_ref, gt_ref, mask_ref, acc, stage, land, res, w1_ref, w2_ref,
    near_send, far_send, strip_recv, red_send, red_recv, load_sem,
):
    depth = x_ref.shape[0]
    half_n = n_space // 2
    used = 3 * depth * tiles
    me = lax.axis_index("space")
    dp = lax.axis_index("dp")
    y = me % 2
    z = me // 2
    core = dp % 2
    x = dp // 2
    mate = z * 2 + (1 - y)
    core_mate = x * 2 + (1 - core)
    x_mate = (1 - x) * 2 + core
    mesh_id = pl.DeviceIdType.MESH
    gath = (gath0, gath1, gath2)

    def peer(q):
        return (z + q) % half_n

    def source(q):
        return (z + half_n - q) % half_n

    load1 = pltpu.make_async_copy(w1_far, w1_ref, load_sem.at[0])
    load2 = pltpu.make_async_copy(w2_far, w2_ref, load_sem.at[1])
    load1.start()
    load2.start()
    barrier = pltpu.get_barrier_semaphore()

    def greet(space_to, dp_to):
        pl.semaphore_signal(barrier, inc=1, device_id=(space_to, dp_to), device_id_type=mesh_id)

    each(half_n - 1, lambda q: greet(peer(q + 1) * 2 + y, dp))
    greet(mate, dp)
    greet(me, core_mate)
    greet(me, x_mate)

    def near_copy(f, q):
        return pltpu.make_async_remote_copy(
            src_ref=gath[f].at[me], dst_ref=gath[f].at[me],
            send_sem=near_send.at[f, q], recv_sem=strip_recv.at[f, me],
            device_id=(peer(q) * 2 + y, dp), device_id_type=mesh_id)

    def far_copy(f, q):
        slot = source(q) * 2 + y
        return pltpu.make_async_remote_copy(
            src_ref=gath[f].at[slot], dst_ref=gath[f].at[slot],
            send_sem=far_send.at[f, q], recv_sem=strip_recv.at[f, slot],
            device_id=(mate, dp), device_id_type=mesh_id)

    def arrived(f, slot):
        pltpu.make_async_remote_copy(
            src_ref=gath[f].at[slot], dst_ref=gath[f].at[slot],
            send_sem=near_send.at[f, 0], recv_sem=strip_recv.at[f, slot],
            device_id=(mate, dp), device_id_type=mesh_id).wait_recv()

    def send_own(f):
        each(half_n - 1, lambda q: near_copy(f, q + 1).start())
        far_copy(f, 0).start()

    def forward(f):
        def step(q):
            arrived(f, source(q + 1) * 2 + y)
            far_copy(f, q + 1).start()
        each(half_n - 1, step)

    def collect(f):
        each(half_n, lambda q: arrived(f, source(q) * 2 + (1 - y)))

    def sent(f):
        def step(q):
            near_copy(f, q + 1).wait_send()
        each(half_n - 1, step)
        each(half_n, lambda q: far_copy(f, q).wait_send())

    j = lax.broadcasted_iota(jnp.int32, (4 * SIDE, CELLS), 0)
    c = lax.broadcasted_iota(jnp.int32, (4 * SIDE, CELLS), 1)
    cell = jnp.where(
        j < SIDE, j,
        jnp.where(j < 2 * SIDE, j + (CELLS - 2 * SIDE),
                  jnp.where(j < 3 * SIDE, (j - 2 * SIDE) * SIDE, (j - 3 * SIDE) * SIDE + SIDE - 1)))
    pick = (c == cell).astype(F32).astype(BF16)

    ocean_row = ocean_ref[...].astype(F32)
    gt = (g_ref[...].astype(F32) * ocean_row).astype(BF16)
    gt_ref[...] = gt
    gath0[me] = matmul(pick, x_ref[...], NT).astype(BF16)
    gath1[me] = matmul(pick, gt, NT).astype(BF16)
    pl.semaphore_wait(barrier, half_n + 2)
    send_own(0)

    ocean_t = jnp.transpose(jnp.broadcast_to(ocean_row, (128, CELLS)))
    mask_ref[...] = jnp.concatenate([ocean_t, ocean_t], axis=1)[:, :depth]

    fold = flag_ref[0]
    ext_row = lax.broadcasted_iota(jnp.int32, (EXT, 3 * SIDE), 0)
    col = lax.broadcasted_iota(jnp.int32, (EXT, 3 * SIDE), 1)
    line = ext_row // SIDE
    spot = ext_row % SIDE
    last = SIDE + 1
    east_col = jnp.where(line == 0, SIDE, jnp.where(line == last, 2 * SIDE, line - 1))
    west_col = jnp.where(line == 0, 2 * SIDE - 1, jnp.where(line == last, 3 * SIDE - 1, line - 1))
    east_put = ((spot == SIDE - 1) & (col == east_col)).astype(F32).astype(BF16)
    west_put = ((spot == 0) & (col == west_col)).astype(F32).astype(BF16)
    nr = lax.broadcasted_iota(jnp.int32, (SIDE, 2 * SIDE), 0)
    nc = lax.broadcasted_iota(jnp.int32, (SIDE, 2 * SIDE), 1)
    north_put = (nc == jnp.where(fold == 1, 2 * SIDE - 1 - nr, nr)).astype(F32).astype(BF16)
    wide = lax.broadcasted_iota(jnp.int32, (EXT, depth), 0) % SIDE

    def build(f, field):
        def block(k, part, count=1):
            index = nb_ref[0, k]
            valid = (index >= 0).astype(F32)
            got = gath[f][jnp.maximum(index, 0), part * SIDE:(part + count) * SIDE, :]
            return got.astype(F32) * valid

        north = matmul(north_put, block(0, 0, 2).astype(BF16))
        south = block(1, 1)
        ext = jnp.concatenate([south, field, north], axis=0)
        east = jnp.concatenate([block(2, 2), block(6, 1), block(4, 0)], axis=0).astype(BF16)
        west = jnp.concatenate([block(3, 3), block(7, 1), block(5, 0)], axis=0).astype(BF16)
        pads[f, 1] = ext.astype(BF16)
        plus = jnp.where(wide == SIDE - 1, 0.0, pltpu.roll(ext, EXT - 1, 0))
        pads[f, 2] = (plus + matmul(east_put, east)).astype(BF16)
        minus = jnp.where(wide == 0, 0.0, pltpu.roll(ext, 1, 0))
        pads[f, 0] = (minus + matmul(west_put, west)).astype(BF16)

    def window(f, dr, dc):
        start = SIDE * (dr + 1)
        return pads[f, dc + 1, start:start + CELLS, :]

    def conv(f, w_ref):
        total = None
        for k in range(9):
            term = matmul(window(f, k // 3 - 1, k % 3 - 1), w_ref[k], NT)
            total = term if total is None else total + term
        return total

    def weight_grad(s, grads, f):
        for dr in range(3):
            parts = [matmul(grads, window(f, dr - 1, dc - 1)) for dc in range(3)]
            spare = jnp.zeros((depth, LANES * tiles - 3 * depth), F32)
            wide = jnp.concatenate(parts + [spare], axis=1)
            for t in range(tiles):
                start = (3 * t + dr) * depth
                acc[s, start:start + depth, :] = wide[:, LANES * t:LANES * (t + 1)]

    by_core = (core, (me, core_mate))
    by_x = (x, (me, x_mate))
    by_y = (y, (mate, dp))
    ways = ((by_core, by_x, by_y), (by_core, by_y, by_x)) * 2
    part = rows // 2
    offsets = []
    for u in range(4):
        off = (u % 2) * part
        marks = []
        for t, (bit, _) in enumerate(ways[u]):
            size = part >> (t + 1)
            marks.append((off + bit * size, off + (1 - bit) * size))
            off = off + bit * size
        offsets.append(marks)
    piece = part // (8 * half_n)

    def span(start, size):
        return pl.ds(pl.multiple_of(start, 16), size)

    def landing(u, t):
        size = part >> (t + 1)
        return pl.ds((u % 2) * part + part - 2 * size, size)

    def halve_copy(u, t):
        return pltpu.make_async_remote_copy(
            src_ref=stage.at[u // 2, span(offsets[u][t][1], part >> (t + 1))],
            dst_ref=land.at[u // 2, landing(u, t)],
            send_sem=red_send.at[u, t], recv_sem=red_recv.at[u, t],
            device_id=ways[u][t][1], device_id_type=mesh_id)

    def halve_start(u, t):
        away = span(offsets[u][t][1], part >> (t + 1))
        stage[u // 2, away] = acc[u // 2, away].astype(BF16)
        halve_copy(u, t).start()

    def halve_end(u, t):
        halve_copy(u, t).wait_recv()
        keep = span(offsets[u][t][0], part >> (t + 1))
        acc[u // 2, keep] = acc[u // 2, keep] + land[u // 2, landing(u, t)].astype(F32)

    def z_land(u, zp):
        return span((u % 2) * part + part - part // 8 + zp * piece, piece)

    def z_copy(u, q):
        off = offsets[u][2][0]
        return pltpu.make_async_remote_copy(
            src_ref=stage.at[u // 2, span(off + peer(q) * piece, piece)],
            dst_ref=land.at[u // 2, z_land(u, z)],
            send_sem=red_send.at[u, 6 + q], recv_sem=red_recv.at[u, 6 + q],
            device_id=(peer(q) * 2 + y, dp), device_id_type=mesh_id)

    def z_start(u):
        whole = span(offsets[u][2][0], part // 8)
        stage[u // 2, whole] = acc[u // 2, whole].astype(BF16)
        each(half_n - 1, lambda q: z_copy(u, q + 1).start())

    def z_end(u):
        mine = span(offsets[u][2][0] + z * piece, piece)

        def step(q):
            z_copy(u, q + 1).wait_recv()
            got = land[u // 2, z_land(u, source(q + 1))]
            acc[u // 2, mine] = acc[u // 2, mine] + got.astype(F32)
        each(half_n - 1, step)
        res[u // 2, mine] = acc[u // 2, mine].astype(BF16)

    def zg_copy(u, q):
        mine = span(offsets[u][2][0] + z * piece, piece)
        return pltpu.make_async_remote_copy(
            src_ref=res.at[u // 2, mine], dst_ref=res.at[u // 2, mine],
            send_sem=red_send.at[u, 6 + half_n + q], recv_sem=red_recv.at[u, 6 + half_n + q],
            device_id=(peer(q) * 2 + y, dp), device_id_type=mesh_id)

    def grow_copy(u, t):
        have = span(offsets[u][t][0], part >> (t + 1))
        return pltpu.make_async_remote_copy(
            src_ref=res.at[u // 2, have], dst_ref=res.at[u // 2, have],
            send_sem=red_send.at[u, 3 + t], recv_sem=red_recv.at[u, 3 + t],
            device_id=ways[u][t][1], device_id_type=mesh_id)

    for s in range(2):
        acc[s, used:] = jnp.zeros((rows - used, LANES), F32)
    forward(0)
    send_own(1)
    field_x = jnp.transpose(x_ref[...].astype(F32))
    collect(0)
    build(0, field_x)
    forward(1)
    load1.wait()
    value, slope = gelu_pair(conv(0, w1_ref))
    hidden = (value * mask_ref[...]).astype(BF16)
    hidden_ref[...] = hidden
    slope_ref[...] = slope * mask_ref[...]
    gath2[me] = matmul(pick, hidden).astype(BF16)
    send_own(2)

    field_g = jnp.transpose(gt_ref[...].astype(F32))
    collect(1)
    build(1, field_g)
    load2.wait()
    forward(2)
    back = None
    edge = None
    for k in (3, 4, 5, 6, 7, 8):
        term = matmul(window(1, 1 - k // 3, 1 - k % 3), w2_ref[k])
        back = term if back is None else back + term
    inner = None
    for k in range(3):
        dc = 1 - k % 3
        term = matmul(pads[1, dc + 1, 2 * SIDE:EXT - SIDE, :], w2_ref[k])
        inner = term if inner is None else inner + term
        across = jnp.where(fold == 1, w2_ref[8 - k].astype(F32), w2_ref[k].astype(F32)).astype(BF16)
        term = matmul(pads[1, dc + 1, EXT - SIDE:EXT, :], across)
        edge = term if edge is None else edge + term
    back = back + jnp.concatenate([inner, edge], axis=0)
    pre_grad = back * slope_ref[...]
    weight_grad(0, jnp.transpose(pre_grad).astype(BF16), 0)
    halve_start(0, 0)
    halve_start(1, 0)

    collect(2)
    build(2, hidden_ref[...].astype(F32))
    for u in (0, 1):
        halve_end(u, 0)
        halve_start(u, 1)
    weight_grad(1, gt_ref[...], 2)
    halve_start(2, 0)
    halve_start(3, 0)
    for u in (0, 1):
        halve_end(u, 1)
        halve_start(u, 2)
    forecast = conv(2, w2_ref) * mask_ref[...]
    for u in (2, 3):
        halve_end(u, 0)
        halve_start(u, 1)
    for u in (0, 1):
        halve_end(u, 2)
        z_start(u)
    pred_ref[...] = jnp.transpose(forecast).astype(BF16)
    for u in (2, 3):
        halve_end(u, 1)
        halve_start(u, 2)

    def finish(u):
        z_end(u)
        each(half_n - 1, lambda q: zg_copy(u, q + 1).start())

    def grow(u, t):
        if t == 2:
            each(half_n - 1, lambda q: zg_copy(u, q + 1).wait_recv())
        else:
            grow_copy(u, t + 1).wait_recv()
        grow_copy(u, t).start()

    def unpack(s, out):
        grow_copy(2 * s, 0).wait_recv()
        grow_copy(2 * s + 1, 0).wait_recv()
        total = res[s].astype(F32)
        for dr in range(3):
            starts = [(3 * t + dr) * depth for t in range(tiles)]
            wide = jnp.concatenate([total[r:r + depth] for r in starts], axis=1)
            for dc in range(3):
                out[3 * dr + dc] = wide[:, dc * depth:(dc + 1) * depth].astype(BF16)

    finish(0)
    finish(1)
    for u in (2, 3):
        halve_end(u, 2)
        z_start(u)
    grow(0, 2)
    grow(1, 2)
    finish(2)
    finish(3)
    grow(0, 1)
    grow(1, 1)
    grow(2, 2)
    grow(3, 2)
    grow(0, 0)
    grow(1, 0)
    grow(2, 1)
    grow(3, 1)
    unpack(0, out1_ref)
    grow(2, 0)
    grow(3, 0)
    unpack(1, out2_ref)
    for f in range(3):
        sent(f)
    for u in range(4):
        for t in range(3):
            halve_copy(u, t).wait_send()
            grow_copy(u, t).wait_send()

        def done(q):
            z_copy(u, q + 1).wait_send()
            zg_copy(u, q + 1).wait_send()
        each(half_n - 1, done)


def body(n_space, input_states, loss_sensitivity, ocean, neighbours, fold_flag, w_first, w_second):
    depth = input_states.shape[2]
    half_n = n_space // 2
    unit = 16 * half_n * 16
    tiles = -(-3 * depth // LANES)
    used = 3 * depth * tiles
    rows = -(-used // unit) * unit
    vmem = pl.BlockSpec(memory_space=pltpu.VMEM)
    smem = pl.BlockSpec(memory_space=pltpu.SMEM)
    hbm = pl.BlockSpec(memory_space=pltpu.HBM)
    prediction, first, second = pl.pallas_call(
        functools.partial(kernel, n_space, rows, tiles),
        out_shape=(
            jax.ShapeDtypeStruct((depth, CELLS), BF16),
            jax.ShapeDtypeStruct((9, depth, depth), BF16),
            jax.ShapeDtypeStruct((9, depth, depth), BF16),
        ),
        in_specs=[vmem, vmem, vmem, smem, smem, hbm, hbm],
        out_specs=(vmem, vmem, vmem),
        scratch_shapes=[
            pltpu.VMEM((n_space, 4 * SIDE, depth), BF16),
            pltpu.VMEM((n_space, 4 * SIDE, depth), BF16),
            pltpu.VMEM((n_space, 4 * SIDE, depth), BF16),
            pltpu.VMEM((3, 3, EXT, depth), BF16),
            pltpu.VMEM((CELLS, depth), BF16),
            pltpu.VMEM((CELLS, depth), F32),
            pltpu.VMEM((depth, CELLS), BF16),
            pltpu.VMEM((CELLS, depth), F32),
            pltpu.VMEM((2, rows, LANES), F32),
            pltpu.VMEM((2, rows, LANES), BF16),
            pltpu.VMEM((2, rows, LANES), BF16),
            pltpu.VMEM((2, rows, LANES), BF16),
            pltpu.VMEM((9, depth, depth), BF16),
            pltpu.VMEM((9, depth, depth), BF16),
            pltpu.SemaphoreType.DMA((3, half_n)),
            pltpu.SemaphoreType.DMA((3, half_n)),
            pltpu.SemaphoreType.DMA((3, n_space)),
            pltpu.SemaphoreType.DMA((4, 6 + 2 * half_n)),
            pltpu.SemaphoreType.DMA((4, 6 + 2 * half_n)),
            pltpu.SemaphoreType.DMA((2,)),
        ],
        compiler_params=pltpu.CompilerParams(
            collective_id=0, has_side_effects=True, vmem_limit_bytes=(32 + n_space // 4) * 1024 * 1024),
    )(input_states[0, 0], loss_sensitivity[0, 0], ocean, neighbours, fold_flag, w_first, w_second)
    return (prediction[None, None], first.astype(F32), second.astype(F32))


def solution(mesh):
    placed = (
        P("dp", "space", None, None),
        P("dp", "space", None, None),
        P("space", None),
        P("space", None),
        P("space"),
        P(),
        P(),
    )
    return jax.shard_map(
        functools.partial(body, mesh.shape["space"]),
        mesh=mesh,
        in_specs=placed,
        out_specs=(P("dp", "space", None, None), P(), P()),
        check_vma=False,
    )
```
